128 devices in a mesh: section: 4 (over y_lo, core), kv: 32 (over y_hi, x, z).
Axes of the slice: x: 4, y: 4 (y_hi: 2, y_lo: 2; y = y_hi * 2 + y_lo), z: 4, core: 2. Of those that a mesh axis runs over, the one named last changes fastest.
Arguments:
- queries: bfloat16 [4, 256, 8192], P('section', 'kv'), may hold values from -20 to 20
- cache_keys: bfloat16 [4, 65536, 1024], P('section', 'kv'), may hold values from -6 to 6
- cache_values: bfloat16 [4, 65536, 1024], P('section', 'kv'), may hold values from -6 to 6
- new_keys: bfloat16 [4, 256, 1024], P('section', 'kv'), may hold values from -6 to 6
- new_values: bfloat16 [4, 256, 1024], P('section', 'kv'), may hold values from -6 to 6
- lengths: int32 [4, 32], P('section', 'kv'), may hold values from 256 to 2048, as said below
- residual: bfloat16 [4, 256, 8192], P('section', 'kv'), may hold values from -6 to 6
Outputs:
- handed: float32 [4, 256, 8192], P('section', 'kv')
- lse: float32 [4, 256, 64], P('section', 'kv')
The draws below stay inside these ranges and needn't reach their ends.
Inputs may be any that keep to these rules, and one draw needn't show every extreme that they name: `lengths`: in every section at least one kv index has all 2048 slots live.
All inputs are finite; a program needn't handle non-finite values.
Results may differ from the reference program's by a relative error of at most 0.0003.
Values may be sent and summed in bfloat16 or wider, within the bound.
A program may use at most 128 MiB of HBM per device.

```python
import jax
import jax.numpy as jnp
from jax import lax

HQ = 64
KVH = 8
HD = 128
D = 8192
QB = 8
CTX_DEV = 2048
SECTIONS = 4
SPAN = 256
CTX = 65536
N_KV = 32


def plant_vector(key):
    folded = jax.random.fold_in(key, 97)
    magnitude = jax.random.uniform(folded, (HD,), jnp.float32, 4.0, 5.5)
    heads = jax.random.bernoulli(jax.random.fold_in(folded, 1), 0.5, (HD,))
    return jnp.where(heads, magnitude, -magnitude)


def plant_plan(key):
    folded = jax.random.fold_in(key, 131)
    row_list = []
    shard_list = []
    for section_index in range(SECTIONS):
        section_key = jax.random.fold_in(folded, section_index)
        picked = jax.random.permutation(section_key, SPAN - 1)[:3] + 1
        offset = jax.random.randint(jax.random.fold_in(section_key, 1), (), 0, N_KV - 1)
        target_shard = (picked[0] // QB + 1 + offset) % N_KV
        row_list.append(picked.astype(jnp.int32))
        shard_list.append(target_shard.astype(jnp.int32))
    return (jnp.stack(row_list), jnp.stack(shard_list))


def key_base(key, rows, tag):
    key = jax.random.fold_in(key, tag)
    return jnp.clip(jax.random.normal(key, (SECTIONS, rows, KVH * HD), jnp.float32), -6.0, 6.0)


def draw_queries(key, part):
    planted = plant_vector(key)
    plant_rows, target_shards = plant_plan(key)
    key = jax.random.fold_in(key, 11)
    base = jnp.clip(3.0 * jax.random.normal(key, (SECTIONS, SPAN, HQ, HD), jnp.float32), -18.0, 18.0)
    strength = jnp.array([120.0, 200.0, 280.0], jnp.float32)
    unit = planted * HD ** 0.5 / jnp.sum(planted * planted)
    for section_index in range(SECTIONS):
        base = base.at[section_index, plant_rows[section_index], 0, :].set(strength[:, None] * unit[None, :])
    return base.reshape(SECTIONS, SPAN, HQ * HD).astype(jnp.bfloat16)


def draw_cache_keys(key, part):
    planted = plant_vector(key)
    plant_rows, target_shards = plant_plan(key)
    base = key_base(key, CTX, 23)
    for section_index in range(SECTIONS):
        first_slot = target_shards[section_index] * CTX_DEV
        base = base.at[section_index, first_slot, 0:HD].set(planted)
        base = base.at[section_index, first_slot + 1, 0:HD].set(0.99 * planted)
    return base.astype(jnp.bfloat16)


def draw_new_keys(key, part):
    planted = plant_vector(key)
    plant_rows, target_shards = plant_plan(key)
    base = key_base(key, SPAN, 37)
    for section_index in range(SECTIONS):
        lowest = jnp.min(plant_rows[section_index])
        base = base.at[section_index, lowest - 1, 0:HD].set(0.6 * planted)
        base = base.at[section_index, lowest, 0:HD].set(0.59 * planted)
    return base.astype(jnp.bfloat16)


def draw_lengths(key, part):
    key = jax.random.fold_in(key, 51)
    spread = jax.random.randint(key, (SECTIONS, N_KV), max(2, CTX_DEV // 8), CTX_DEV + 1)
    fullest = jax.random.randint(jax.random.fold_in(key, 1), (SECTIONS, 1), 0, N_KV)
    column = jnp.arange(N_KV, dtype=jnp.int32)[None, :]
    return jnp.where(column == fullest, CTX_DEV, spread).astype(jnp.int32)


def block_scale(own_key, extent, shards, low, top_value):
    factor_of = 1.0
    for position, blocks in shards:
        draws = jax.random.uniform(jax.random.fold_in(jax.random.fold_in(own_key, 6), position), (blocks,), jnp.float32, low / len(shards), top_value / len(shards))
        factor_of = factor_of * jnp.repeat(jnp.exp(draws), extent[position] // blocks).reshape((-1,) + (1,) * (len(extent) - 1 - position))
    return factor_of


def normal_values(key, dims, scale, bound, split=(), kind=jnp.bfloat16):
    factor_of = block_scale(key, dims, split, -0.22, 0.18) if split else 1.0
    result = jax.random.normal(key, dims, jnp.float32) * scale * factor_of
    return jnp.minimum(jnp.maximum(result, -bound), bound).astype(kind)


def setup_inputs(seed: int = 0) -> dict:
    key_of = jax.random.split(jax.random.key(seed), 8)
    queries = draw_queries(jax.random.fold_in(key_of[7], 71), 0)
    cache_keys = draw_cache_keys(jax.random.fold_in(key_of[7], 71), 0)
    cache_values = normal_values(key_of[2], (SECTIONS, CTX, KVH * HD), 1.0, 6.0, ((0, 4), (1, 32)))
    new_keys = draw_new_keys(jax.random.fold_in(key_of[7], 71), 0)
    new_values = normal_values(key_of[4], (SECTIONS, SPAN, KVH * HD), 1.0, 6.0, ((0, 4), (1, 32)))
    lengths = draw_lengths(jax.random.fold_in(key_of[7], 71), 0)
    residual = normal_values(key_of[6], (SECTIONS, SPAN, D), 1.0, 6.0, ((0, 4), (1, 32)))
    return {"queries": queries, "cache_keys": cache_keys, "cache_values": cache_values, "new_keys": new_keys, "new_values": new_values, "lengths": lengths, "residual": residual}


def attend(group_queries, group_keys, group_values, valid):
    scale = HD ** -0.5
    scores = jnp.einsum('qhd,kd->hqk', group_queries.astype(jnp.float32), group_keys.astype(jnp.float32)) * scale
    scores = jnp.where(valid[None], scores, -1e30)
    top = jnp.max(scores, axis=2, keepdims=True)
    weights = jnp.exp(scores - top)
    total = jnp.sum(weights, axis=2)
    rounded = weights.astype(jnp.bfloat16).astype(jnp.float32)
    mixed = jnp.einsum('hqk,kd->qhd', rounded, group_values.astype(jnp.float32))
    normed = mixed / jnp.transpose(total)[:, :, None]
    return normed, jnp.transpose(top[:, :, 0] + jnp.log(total))


def shard_partial(block_queries, keys, values, valid):
    rows = block_queries.shape[0]
    per_group = HQ // KVH
    query4 = block_queries.reshape(rows, KVH, per_group, HD)
    keys3 = keys.reshape(keys.shape[0], KVH, HD)
    values3 = values.reshape(values.shape[0], KVH, HD)

    def one_group(group):
        group_queries = lax.dynamic_index_in_dim(query4, group, 1, False)
        group_keys = lax.dynamic_index_in_dim(keys3, group, 1, False)
        group_values = lax.dynamic_index_in_dim(values3, group, 1, False)
        return attend(group_queries, group_keys, group_values, valid)

    normed, lses = lax.map(one_group, jnp.arange(KVH).astype(jnp.int32))
    normed = jnp.transpose(normed, (1, 0, 2, 3)).reshape(rows, HQ * HD)
    lses = jnp.transpose(lses, (1, 0, 2)).reshape(rows, HQ)
    return normed, lses


def one_section(inputs):
    block_queries, keys, values, fresh_keys, fresh_values, section_lengths = inputs

    def one_shard(shard):
        begin = (shard * CTX_DEV).astype(jnp.int32)
        shard_keys = lax.dynamic_slice_in_dim(keys, begin, CTX_DEV, 0)
        shard_values = lax.dynamic_slice_in_dim(values, begin, CTX_DEV, 0)
        live = lax.dynamic_index_in_dim(section_lengths, shard, 0, False)
        valid = (jnp.arange(CTX_DEV) < live)[None, :]
        return shard_partial(block_queries, shard_keys, shard_values, valid)

    parts, part_lses = lax.map(one_shard, jnp.arange(N_KV).astype(jnp.int32))
    causal = jnp.arange(SPAN)[None, :] <= jnp.arange(SPAN)[:, None]
    own_part, own_lse = shard_partial(block_queries, fresh_keys, fresh_values, causal)
    every_part = jnp.concatenate([parts, own_part[None]], axis=0)
    every_lse = jnp.concatenate([part_lses, own_lse[None]], axis=0)
    peak = jnp.max(every_lse, axis=0)
    joint = peak + jnp.log(jnp.sum(jnp.exp(every_lse - peak[None]), axis=0))
    shares = jnp.exp(every_lse - joint[None])
    stacked = every_part.reshape(N_KV + 1, SPAN, HQ, HD)
    attn = jnp.sum(shares[..., None] * stacked, axis=0).reshape(SPAN, HQ * HD)
    return attn, joint


def reference(queries, cache_keys, cache_values, new_keys, new_values, lengths, residual):
    attn, joint = lax.map(one_section, (queries, cache_keys, cache_values, new_keys, new_values, lengths))
    updated = residual.astype(jnp.float32) + attn
    handed = jnp.roll(updated, 1, axis=0)
    return handed, joint
```

```python
import functools

import jax
import jax.numpy as jnp
from jax import lax
from jax.experimental import pallas as pl
from jax.experimental.pallas import tpu as pltpu
from jax.sharding import PartitionSpec as P

MESH = pl.DeviceIdType.MESH
F32, BF16, I16 = jnp.float32, jnp.bfloat16, jnp.int16

HQ, KVH, HD, QB = 64, 8, 128, 8
GH = 4
ROWS = 64
BLK = 80
CTX = 2048
UROWS = 256
NKV = 32
SLOTS = NKV + 4
SCALE = HD**-0.5
LOG2E = 1.4426950408889634
CODE = 32700.0
LOW = -1e30


def kernel(
    len_ref, q_ref, nk_ref, nv_ref, res_ref, k_hbm, v_hbm,
    out_ref, lse_ref,
    ga, kraw, vt, vv, bias, po, pa, bp, ba, rp, rb, ra, resb, rres, lsend, lrecv, notes, inv2, s0, s1, p0, p1, mx,
    kv_sem, g1s, g1r, g2s, g2r, g3s, g3r, u2s, u2r, v2s, v2r, b2s, b2r, rss, rsr, lss, lsr,
):
    s = lax.axis_index("section")
    me = lax.axis_index("kv")
    y, x, z = me // 16, (me // 4) % 4, me % 4
    nxt, prv = (s + 1) % 4, (s + 3) % 4
    here = (me, y * 16 + z * 4 + x)
    along = (x, z)
    within = (z, x)

    def line_pos(yy, a):
        return yy * 16 + a * 4

    def device(half, yy, a, w):
        return yy * 16 + jnp.where(half == 0, a * 4 + w, w * 4 + a)

    def pick(half, pair):
        return jnp.where(half == 0, pair[0], pair[1])

    load_k = pltpu.make_async_copy(k_hbm, kraw, kv_sem.at[0])
    load_v = pltpu.make_async_copy(v_hbm, vv, kv_sem.at[1])
    load_k.start()
    load_v.start()

    bar = pltpu.get_barrier_semaphore()

    def greet(sec, kv):
        pl.semaphore_signal(bar, inc=1, device_id=(sec, kv), device_id_type=MESH)

    for half in range(2):
        for dy in range(2):
            for d in range(4):
                if (dy, d) != (0, 0) and not (half == 1 and d == 0):
                    greet(s, device(half, (y + dy) % 2, along[half], (within[half] + d) % 4))

    def greet_all(i, c):
        greet(prv, i)
        return c

    lax.fori_loop(0, NKV, greet_all, 0)
    greet(nxt, me)

    for half in range(2):
        for gl in range(GH):
            g = half * GH + gl
            for pair in range(4):
                c0 = (g * 8 + pair * 2) * HD
                two = jnp.concatenate(
                    [q_ref[:, c0 : c0 + HD].astype(F32), q_ref[:, c0 + HD : c0 + 2 * HD].astype(F32)], axis=0
                )
                ga[half * NKV + here[half], gl, pair * 16 : pair * 16 + 16, :] = two.astype(BF16)
            cols = slice(g * HD, g * HD + HD)
            two = jnp.concatenate([nk_ref[:, cols].astype(F32), nv_ref[:, cols].astype(F32)], axis=0)
            ga[half * NKV + here[half], gl, ROWS:BLK, :] = two.astype(BF16)
    resb[...] = res_ref[...].astype(F32)

    pl.semaphore_wait(bar, 13 + NKV + 1)

    def send_block(half, dy, d):
        at = ga.at[half * NKV + here[half]]
        pltpu.make_async_remote_copy(
            src_ref=at,
            dst_ref=at,
            send_sem=g1s,
            recv_sem=g1r.at[half, dy],
            device_id=(s, device(half, (y + dy) % 2, along[half], (within[half] + d) % 4)),
            device_id_type=MESH,
        ).start()

    for dy in range(2):
        for d in (1, 3, 2, 0):
            for half in range(2):
                if (dy, d) != (0, 0):
                    send_block(half, dy, d)

    residual = pltpu.make_async_remote_copy(
        src_ref=resb, dst_ref=rres, send_sem=rss, recv_sem=rsr, device_id=(nxt, me), device_id_type=MESH
    )

    slot = lax.broadcasted_iota(jnp.int32, (CTX, HD), 0)
    first = lax.broadcasted_iota(jnp.int32, (CTX, HD), 1) == 0
    bias[...] = jnp.where(first & (slot >= len_ref[0, 0]), LOW, 0.0).astype(BF16)
    load_v.wait()

    def turn(g, c):
        vt[g] = vv[:, pl.ds(pl.multiple_of(g * HD, HD), HD)].T
        return c

    lax.fori_loop(0, KVH, turn, 0)

    def send_line(half, yy, a, to):
        base = half * NKV + line_pos(yy, a)
        copies = (
            (ga.at[pl.ds(base, 4), :, 0:ROWS], g2s, g2r.at[half, yy * 4 + a]),
            (ga.at[pl.ds(base, 4), within[half], ROWS:BLK], g3s, g3r.at[half, yy * 4 + a]),
        )
        for at, send_sem, recv_sem in copies:
            pltpu.make_async_remote_copy(
                src_ref=at,
                dst_ref=at,
                send_sem=send_sem,
                recv_sem=recv_sem,
                device_id=(s, device(half, y, to, within[half])),
                device_id_type=MESH,
            ).start()

    def first_wait(half, dy):
        blocks = ga.at[pl.ds(0, 4 if dy else 3)]
        pltpu.make_async_copy(blocks, blocks, g1r.at[half, dy]).wait()
        yy, a = (y + dy) % 2, along[half]
        send_line(half, yy, a, (a + 1) % 4)
        send_line(half, yy, a, (a + 3) % 4)

    def line_wait(half, yy, a):
        blocks = ga.at[pl.ds(half * NKV + line_pos(yy, a), 4), :, 0:ROWS]
        pltpu.make_async_copy(blocks, blocks, g2r.at[half, yy * 4 + a]).wait()
        blocks = ga.at[pl.ds(half * NKV + line_pos(yy, a), 4), within[half], ROWS:BLK]
        pltpu.make_async_copy(blocks, blocks, g3r.at[half, yy * 4 + a]).wait()

    first_wait(0, 0)
    first_wait(1, 0)

    lane = lax.broadcasted_iota(jnp.int32, (UROWS, HD), 1)

    blank = jnp.zeros((4 * ROWS, HD), BF16)
    lane4 = lane[0 : 4 * ROWS]

    def coded(o):
        r = jnp.maximum(jnp.max(jnp.abs(o), axis=1, keepdims=True), 1e-30)
        inv = pl.reciprocal(r, approx=True) * CODE
        return jnp.round(o * inv).astype(jnp.int32).astype(I16), inv

    def packed(stats):
        total = stats[GH : 2 * GH]
        lse = stats[0:GH] * SCALE + jnp.log(total)
        return jnp.concatenate([lse, 1.0 / (stats[2 * GH : 3 * GH] * total)], axis=0)

    def noted(gl, lanes, m, total, inv, before):
        return jnp.where(
            lanes == gl, m, jnp.where(lanes == GH + gl, total, jnp.where(lanes == 2 * GH + gl, inv, before))
        )

    def send_to(src, dst, send_sem, recv_sem, to):
        pltpu.make_async_remote_copy(
            src_ref=src, dst_ref=dst, send_sem=send_sem, recv_sem=recv_sem, device_id=to, device_id_type=MESH
        ).start()

    def send_block_out(half, base, w, yy, a):
        slot = pick(half, here)
        to = (nxt, device(half, yy, a, w))
        send_to(po.at[base + w], rp.at[half * NKV + slot], u2s, u2r.at[half], to)
        send_to(pa.at[base + w], ra.at[half * SLOTS + slot], b2s, b2r, to)

    def own_block(accs):
        mine = lax.broadcasted_iota(jnp.int32, (8, HD), 0)

        def one(half, c):
            w, a = pick(half, within), pick(half, along)
            base = half * NKV + line_pos(y, a)
            col = lax.broadcasted_iota(jnp.int32, (4 * ROWS, NKV * 16), 1)
            row = lax.broadcasted_iota(jnp.int32, (4 * ROWS, NKV * 16), 0)
            p = col // 16
            src = jnp.where(half == 0, p, (p // 16) * 16 + (p % 4) * 4 + (p // 4) % 4)
            dst = device(half, y, a, row // ROWS)
            allowed = (col % 16 < QB) & (src * QB + col % 16 <= dst * QB + row % QB)
            kv = ga[pl.ds(half * NKV, NKV), w, ROWS:BLK, :].reshape(NKV * 16, HD)
            q = ga[pl.ds(base, 4), w, 0:ROWS, :].reshape(4 * ROWS, HD)
            tiles = [jnp.concatenate([kv[j * 256 : (j + 1) * 256], blank], axis=1) for j in range(2)]
            q = jnp.concatenate([q, blank], axis=1)
            for j in range(2):
                pltpu.matmul_push_rhs(tiles[j], j, 0, transpose=True)
                pltpu.matmul_acc_lhs(accs[j], q, load_staged_rhs=j)
            sc = [pltpu.matmul_pop(accs[j]) for j in range(2)]
            sc = jnp.where(allowed, jnp.concatenate(sc, axis=1), LOW)
            m = jnp.max(sc, axis=1, keepdims=True)
            e = jnp.where(allowed, jnp.exp2((sc - m) * (SCALE * LOG2E)), 0.0)
            total = jnp.sum(e, axis=1, keepdims=True)
            e = pltpu.roll(e, 8, 1).astype(BF16)
            for j in range(2):
                pltpu.matmul_push_rhs(tiles[j], j, 1)
                pltpu.matmul_acc_lhs(accs[2], e[:, j * 256 : (j + 1) * 256], load_staged_rhs=j)
            o = pltpu.matmul_pop(accs[2])[:, 0:HD]
            code, inv = coded(o)
            bp[half] = code.reshape(4, ROWS, HD)
            inv2[...] = noted(w, lane4, m, total, inv, jnp.ones((4 * ROWS, HD), F32))
            for two in range(2):
                flat = packed(inv2[two * 2 * ROWS : (two + 1) * 2 * ROWS, :].T)
                flat = jnp.where(mine % GH == w, flat, jnp.where(mine < GH, LOW, 0.0))
                ba[half, 2 * two] = flat
                ba[half, 2 * two + 1] = pltpu.roll(flat, ROWS, 1)
            for b in range(4):
                to = (nxt, device(half, y, a, b))
                send_to(bp.at[half, b], rb.at[half, w], v2s, v2r.at[half], to)
                send_to(ba.at[half, b], ra.at[half * SLOTS + NKV + w], b2s, b2r, to)
            return c

        lax.fori_loop(0, 2, one, 0)

    def order(t):
        q = t // 2
        dy = jnp.where((q == 1) | (q == 3) | (q == 4) | (q == 7), 1, 0)
        off = jnp.where(q < 2, 0, jnp.where((q == 2) | (q == 4), 3, jnp.where((q == 3) | (q == 5), 1, 2)))
        return t % 2, (y + dy) % 2, off

    def bases_of(t):
        half, yy, off = order(t)
        return (half * NKV + line_pos(yy, (pick(half, along) + off) % 4),)

    def arrived(t):
        half, yy, off = order(t)
        y2 = (y + 1) % 2

        @pl.when(t == 1)
        def _():
            first_wait(0, 1)
            first_wait(1, 1)

        for h in range(2):

            @pl.when((t >= 4) & (half == h))
            def _():
                a = along[h]
                line_wait(h, yy, (a + off) % 4)

                @pl.when(t // 2 == 2)
                def _():
                    send_line(h, y, (a + 3) % 4, (a + 1) % 4)

                @pl.when(t // 2 == 3)
                def _():
                    send_line(h, y2, (a + 1) % 4, (a + 3) % 4)

        @pl.when(t == 10)
        def _():
            residual.start()

    ss, pp = (s0, s1), (p0, p1)
    TILE, CHUNK, STEPS = 256, 32, 8
    ones = jnp.where(lane == 0, 1.0, 0.0).astype(BF16)

    def scores_rhs(bases, gl):
        q = ga[pl.ds(bases[0], 4), gl, 0:ROWS, :].reshape(UROWS, HD)
        pltpu.matmul_push_rhs(jnp.concatenate([q, ones], axis=1), gl % 2, 0, transpose=True)

    def scores_lhs(j, g):
        rows = slice(j * TILE, (j + 1) * TILE)
        return jnp.concatenate([kraw[rows, pl.ds(pl.multiple_of(g * HD, HD), HD)], bias[rows, :]], axis=1)

    def values_push(j, buf):
        pltpu.matmul_push_rhs(pp[buf][j * TILE : (j + 1) * TILE, :], j % 2, 1)

    def values_lhs(j, g):
        return vt[g, :, j * TILE : (j + 1) * TILE]

    def scores_end(j, acc, buf):
        tile = pltpu.matmul_pop(acc)
        ss[buf][j * TILE : (j + 1) * TILE, :] = tile
        high = jnp.max(tile.reshape(TILE // 8, 8, UROWS), axis=0)
        mx[buf] = high if j == 0 else jnp.maximum(mx[buf], high)

    def softmax_chunk(j, m, total, buf):
        rows = slice(j * TILE, (j + 1) * TILE)
        w = jnp.exp2((ss[buf][rows, :] - m) * (SCALE * LOG2E))
        pp[buf][rows, :] = w.astype(BF16)
        added = jnp.sum(w.reshape(TILE // 8, 8, UROWS), axis=0)
        return added if total is None else total + added

    def softmax_end(m, total, gl, turn):
        total = jnp.sum(total, axis=0, keepdims=True)
        notes[turn, gl : gl + 1, :] = m * SCALE + jnp.log(total)
        notes[turn, 2 * GH + gl : 2 * GH + gl + 1, :] = total

    def values_end(o, bases, gl, turn):
        inv = CODE / jnp.maximum(jnp.max(jnp.abs(o), axis=0, keepdims=True), 1e-30)
        code = jnp.round((o * inv).T).astype(jnp.int32).astype(I16)
        po[pl.ds(bases[0], 4), gl] = code.reshape(4, ROWS, HD)
        notes[turn, GH + gl : GH + gl + 1, :] = 1.0 / (inv * notes[turn, 2 * GH + gl : 2 * GH + gl + 1, :])

    def step(accs, after, now, before, pending):
        gl = now[3]
        buf, other = gl % 2, 1 - gl % 2
        score, value = accs[0:2], accs[3 + other]
        g_a, g_b = after[1] * GH + after[3], before[1] * GH + before[3]
        scores_rhs(after[0], after[3])
        values_push(0, other)
        m = total = None
        for j in range(STEPS):
            pltpu.matmul_acc_lhs(score[j % 2], scores_lhs(j, g_a), load_staged_rhs=after[3] % 2 if j == 0 else None)
            pltpu.matmul_acc_lhs(value, values_lhs(j, g_b), load_staged_rhs=j % 2)
            if j == 0:
                for todo in pending:
                    todo()
                m = jnp.max(mx[buf], axis=0, keepdims=True)
            if j + 1 < STEPS:
                values_push(j + 1, other)
            total = softmax_chunk(j, m, total, buf)
            if j > 0:
                scores_end(j - 1, score[(j - 1) % 2], other)
        softmax_end(m, total, gl, now[2])

        def last_tile():
            scores_end(STEPS - 1, score[(STEPS - 1) % 2], other)

        def values():
            values_end(pltpu.matmul_pop(value), before[0], before[3], before[2])

        return last_tile, values

    def pack_notes(bases, turn):
        for pair in range(2):
            flat = notes[turn, 0 : 2 * GH, pair * HD : (pair + 1) * HD]
            pa[bases[0] + 2 * pair] = flat
            pa[bases[0] + 2 * pair + 1] = pltpu.roll(flat, ROWS, 1)

    def send_unit(t):
        half, yy, off = order(t)

        @pl.when(t >= 0)
        def _():
            for w in range(4):
                send_block_out(half, bases_of(t)[0], w, yy, (pick(half, along) + off) % 4)

    def unit(accs, t, c):
        arrived(t)

        @pl.when(t == 15)
        def _():
            own_block(accs)

        tb = jnp.maximum(t - 1, 0)
        new = lambda gl: (bases_of(t), t % 2, t % 2, gl)
        old = lambda gl: (bases_of(tb), tb % 2, (t + 1) % 2, gl)
        todo = step(accs, new(0), old(3), old(2), ())
        todo = step(accs, new(1), new(0), old(3), todo)
        for last in todo:
            last()
        pack_notes(bases_of(tb), (t + 1) % 2)
        send_unit(t - 1)
        todo = step(accs, new(2), new(1), new(0), ())
        todo = step(accs, new(3), new(2), new(1), todo)
        for last in todo:
            last()
        return c

    load_k.wait()
    for ref in (p0, p1):
        ref[...] = jnp.zeros((CTX, UROWS), BF16)
    s1[...] = jnp.zeros((CTX, UROWS), F32)
    mx[...] = jnp.zeros((2, 8, UROWS), F32)
    notes[...] = jnp.ones((2, 16, UROWS), F32)

    def units(*accs):
        lax.fori_loop(0, 16, functools.partial(unit, accs), 0)
        bases, value = bases_of(15), accs[3]
        m, total = jnp.max(mx[1], axis=0, keepdims=True), None
        for j in range(STEPS):
            values_push(j, 0)
            pltpu.matmul_acc_lhs(value, values_lhs(j, 6), load_staged_rhs=j % 2)
            total = softmax_chunk(j, m, total, 1)
        softmax_end(m, total, 3, 1)
        values_end(pltpu.matmul_pop(value), bases, 2, 1)
        for j in range(STEPS):
            values_push(j, 1)
            pltpu.matmul_acc_lhs(value, values_lhs(j, 7), load_staged_rhs=j % 2)
        values_end(pltpu.matmul_pop(value), bases, 3, 1)

    shapes = ((0, UROWS), (0, UROWS), (1, UROWS), (1, HD), (1, HD))
    pl.run_scoped(units, *(pltpu.ACC(one)((size, 2 * HD), F32) for one, size in shapes))
    pack_notes(bases_of(15), 1)
    send_unit(15)

    pltpu.make_async_copy(ra, ra, b2r).wait()
    cols = lax.broadcasted_iota(jnp.int32, (QB, HD), 1)
    lout = jnp.zeros((QB, HD), F32)
    for half in range(2):
        lses = ra[half * SLOTS : (half + 1) * SLOTS, 0:GH, :]
        top = jnp.max(lses, axis=0, keepdims=True)
        lse = top + jnp.log(jnp.sum(jnp.exp(lses - top), axis=0, keepdims=True))
        ra[half * SLOTS : (half + 1) * SLOTS, 0:GH, :] = (
            jnp.exp(lses - lse) * ra[half * SLOTS : (half + 1) * SLOTS, GH : 2 * GH, :]
        )
        flat = jnp.concatenate([lse[0], jnp.zeros((HD - GH, HD), F32)], axis=0).T
        for gl in range(GH):
            for h in range(8):
                piece = flat[h * QB : (h + 1) * QB, gl : gl + 1]
                lout = jnp.where(cols == (half * GH + gl) * 8 + h, piece, lout)
    lsend[...] = lout
    back = pltpu.make_async_remote_copy(
        src_ref=lsend, dst_ref=lrecv, send_sem=lss, recv_sem=lsr, device_id=(prv, me), device_id_type=MESH
    )
    back.start()
    residual.wait_recv()

    for half in range(2):
        parts = rp.at[pl.ds(half * NKV, NKV)]
        pltpu.make_async_copy(parts, parts, u2r.at[half]).wait()
        pltpu.make_async_copy(rb.at[half], rb.at[half], v2r.at[half]).wait()

        def add(n, acc):
            factors = ra[pl.ds(half * SLOTS + n * 16, 16)].reshape(HD, HD).T
            for i in range(16):
                part = rp[half * NKV + n * 16 + i]
                acc = tuple(
                    acc[gl]
                    + part[gl].astype(jnp.int32).astype(F32) * factors[0:ROWS, i * 8 + gl : i * 8 + gl + 1]
                    for gl in range(GH)
                )
            return acc

        acc = lax.fori_loop(0, 2, add, tuple(jnp.zeros((ROWS, HD), F32) for _ in range(GH)))
        rows = ra[half * SLOTS + NKV : (half + 1) * SLOTS].reshape(32, HD)
        factors = jnp.concatenate([rows, jnp.zeros((HD - 32, HD), F32)], axis=0).T
        acc = [
            acc[gl] + rb[half, gl].astype(jnp.int32).astype(F32) * factors[0:ROWS, gl * 9 : gl * 9 + 1]
            for gl in range(GH)
        ]
        for gl in range(GH):
            for h in range(8):
                c0 = ((half * GH + gl) * 8 + h) * HD
                out_ref[:, c0 : c0 + HD] = rres[:, c0 : c0 + HD] + acc[gl][h * QB : (h + 1) * QB, :]

    back.wait_recv()
    lse_ref[...] = lrecv[:, 0:HQ]
    back.wait_send()
    residual.wait_send()
    blocks = ga.at[pl.ds(0, 14)]
    pltpu.make_async_copy(blocks, blocks, g1s).wait()
    blocks = ga.at[pl.ds(0, 48), :, 0:ROWS]
    pltpu.make_async_copy(blocks, blocks, g2s).wait()
    blocks = ga.at[pl.ds(0, 48), 0, ROWS:BLK]
    pltpu.make_async_copy(blocks, blocks, g3s).wait()
    for ref, sem in ((po, u2s), (bp, v2s), (ra, b2s)):
        pltpu.make_async_copy(ref, ref, sem).wait()


def per_device(queries, cache_keys, cache_values, new_keys, new_values, lengths, residual):
    vmem = pl.BlockSpec(memory_space=pltpu.VMEM)
    hbm = pl.BlockSpec(memory_space=pl.ANY)
    dma = pltpu.SemaphoreType.DMA
    handed, lse = pl.pallas_call(
        kernel,
        out_shape=(jax.ShapeDtypeStruct((QB, HQ * HD), F32), jax.ShapeDtypeStruct((QB, HQ), F32)),
        in_specs=[pl.BlockSpec(memory_space=pltpu.SMEM), vmem, vmem, vmem, vmem, hbm, hbm],
        out_specs=(vmem, vmem),
        scratch_shapes=[
            pltpu.VMEM((2 * NKV, GH, BLK, HD), BF16),
            pltpu.VMEM((CTX, KVH * HD), BF16),
            pltpu.VMEM((KVH, HD, CTX), BF16),
            pltpu.VMEM((CTX, KVH * HD), BF16),
            pltpu.VMEM((CTX, HD), BF16),
            pltpu.VMEM((2 * NKV, GH, ROWS, HD), I16),
            pltpu.VMEM((2 * NKV, 8, HD), F32),
            pltpu.VMEM((2, 4, ROWS, HD), I16),
            pltpu.VMEM((2, 4, 8, HD), F32),
            pltpu.VMEM((2 * NKV, GH, ROWS, HD), I16),
            pltpu.VMEM((2, GH, ROWS, HD), I16),
            pltpu.VMEM((2 * SLOTS, 8, HD), F32),
            pltpu.VMEM((QB, HQ * HD), F32),
            pltpu.VMEM((QB, HQ * HD), F32),
            pltpu.VMEM((QB, HD), F32),
            pltpu.VMEM((QB, HD), F32),
            pltpu.VMEM((2, 16, UROWS), F32),
            pltpu.VMEM((4 * ROWS, HD), F32),
            pltpu.VMEM((CTX, UROWS), F32),
            pltpu.VMEM((CTX, UROWS), F32),
            pltpu.VMEM((CTX, UROWS), BF16),
            pltpu.VMEM((CTX, UROWS), BF16),
            pltpu.VMEM((2, 8, UROWS), F32),
            dma((2,)),
            dma,
            dma((2, 2)),
            dma,
            dma((2, 8)),
            dma,
            dma((2, 8)),
            dma,
            dma((2,)),
            dma,
            dma((2,)),
            dma,
            dma,
            dma,
            dma,
            dma,
            dma,
        ],
        compiler_params=pltpu.CompilerParams(
            collective_id=0, has_side_effects=True, vmem_limit_bytes=60 * 1024 * 1024
        ),
        cost_estimate=pl.CostEstimate(
            flops=4 * HQ * 256 * CTX * HD, bytes_accessed=12 * 1024 * 1024, transcendentals=HQ * 256 * CTX
        ),
    )(lengths, queries[0], new_keys[0], new_values[0], residual[0], cache_keys[0], cache_values[0])
    return handed[None], lse[None]


def solution(mesh):
    rows = P("section", "kv", None)
    return jax.shard_map(
        per_device,
        mesh=mesh,
        in_specs=(rows, rows, rows, rows, rows, P("section", "kv"), rows),
        out_specs=(rows, rows),
        check_vma=False,
    )
```

```python
import functools

import jax
import jax.numpy as jnp
from jax import lax
from jax.experimental import pallas as pl
from jax.experimental.pallas import tpu as pltpu
from jax.sharding import PartitionSpec as P

MESH = pl.DeviceIdType.MESH
F32, BF16, I16 = jnp.float32, jnp.bfloat16, jnp.int16

HQ, KVH, HD, QB = 64, 8, 128, 8
GH = 4
ROWS = 64
BLK = 80
CTX = 2048
UROWS = 256
NKV = 32
SLOTS = 8
SCALE = HD**-0.5
LOG2E = 1.4426950408889634
CODE = 32700.0
LOW = -1e30


def kernel(
    len_ref, q_ref, nk_ref, nv_ref, res_ref, k_hbm, v_hbm,
    out_ref, lse_ref,
    ga, kraw, vt, vv, bias, po, pa, r1, a1, bp, ba, po2, pa2, rp, ra, resb, rres, lsend, lrecv, notes, inv2, s0, s1, p0, p1, mx,
    kv_sem, g1s, g1r, g2s, g2r, g3s, g3r, u1s, u1r, b1s, b1r, u2s, u2r, b2s, b2r, rss, rsr, lss, lsr,
):
    s = lax.axis_index("section")
    me = lax.axis_index("kv")
    y, x, z = me // 16, (me // 4) % 4, me % 4
    nxt, prv = (s + 1) % 4, (s + 3) % 4
    here = (me, y * 16 + z * 4 + x)
    along = (x, z)
    within = (z, x)

    def line_pos(yy, a):
        return yy * 16 + a * 4

    def device(half, yy, a, w):
        return yy * 16 + jnp.where(half == 0, a * 4 + w, w * 4 + a)

    def pick(half, pair):
        return jnp.where(half == 0, pair[0], pair[1])

    load_k = pltpu.make_async_copy(k_hbm, kraw, kv_sem.at[0])
    load_v = pltpu.make_async_copy(v_hbm, vv, kv_sem.at[1])
    load_k.start()
    load_v.start()

    bar = pltpu.get_barrier_semaphore()

    def greet(sec, kv):
        pl.semaphore_signal(bar, inc=1, device_id=(sec, kv), device_id_type=MESH)

    for half in range(2):
        for dy in range(2):
            for d in range(4):
                if (dy, d) != (0, 0) and not (half == 1 and d == 0):
                    greet(s, device(half, (y + dy) % 2, along[half], (within[half] + d) % 4))

    for half in range(2):
        for yy in range(2):
            for w in range(4):
                if half == 0:
                    greet(prv, device(0, yy, x, w))
                else:

                    @pl.when(w != x)
                    def _():
                        greet(prv, device(1, yy, z, w))

    greet(nxt, me)

    for half in range(2):
        for gl in range(GH):
            g = half * GH + gl
            for pair in range(4):
                c0 = (g * 8 + pair * 2) * HD
                two = jnp.concatenate(
                    [q_ref[:, c0 : c0 + HD].astype(F32), q_ref[:, c0 + HD : c0 + 2 * HD].astype(F32)], axis=0
                )
                ga[half * NKV + here[half], gl, pair * 16 : pair * 16 + 16, :] = two.astype(BF16)
            cols = slice(g * HD, g * HD + HD)
            two = jnp.concatenate([nk_ref[:, cols].astype(F32), nv_ref[:, cols].astype(F32)], axis=0)
            ga[half * NKV + here[half], gl, ROWS:BLK, :] = two.astype(BF16)
    resb[...] = res_ref[...].astype(F32)

    pl.semaphore_wait(bar, 13 + 14 + 1)

    def send_block(half, dy, d):
        at = ga.at[half * NKV + here[half]]
        pltpu.make_async_remote_copy(
            src_ref=at,
            dst_ref=at,
            send_sem=g1s,
            recv_sem=g1r.at[half, dy],
            device_id=(s, device(half, (y + dy) % 2, along[half], (within[half] + d) % 4)),
            device_id_type=MESH,
        ).start()

    for dy in range(2):
        for d in (1, 3, 2, 0):
            for half in range(2):
                if (dy, d) != (0, 0):
                    send_block(half, dy, d)

    residual = pltpu.make_async_remote_copy(
        src_ref=resb, dst_ref=rres, send_sem=rss, recv_sem=rsr, device_id=(nxt, me), device_id_type=MESH
    )

    slot = lax.broadcasted_iota(jnp.int32, (CTX, HD), 0)
    first = lax.broadcasted_iota(jnp.int32, (CTX, HD), 1) == 0
    bias[...] = jnp.where(first & (slot >= len_ref[0, 0]), LOW, 0.0).astype(BF16)
    load_v.wait()

    def turn(g, c):
        vt[g] = vv[:, pl.ds(pl.multiple_of(g * HD, HD), HD)].T
        return c

    lax.fori_loop(0, KVH, turn, 0)

    def send_line(half, yy, a, to):
        blocks = pl.ds(half * NKV + line_pos(yy, a), 4)
        for at, send_sem, recv_sem in (
            (ga.at[blocks, :, 0:ROWS], g2s, g2r.at[half, yy * 4 + a]),
            (ga.at[blocks, within[half], ROWS:BLK], g3s, g3r.at[half, yy * 4 + a]),
        ):
            pltpu.make_async_remote_copy(
                src_ref=at,
                dst_ref=at,
                send_sem=send_sem,
                recv_sem=recv_sem,
                device_id=(s, device(half, y, to, within[half])),
                device_id_type=MESH,
            ).start()

    def first_wait(half, dy):
        blocks = ga.at[pl.ds(0, 4 if dy else 3)]
        pltpu.make_async_copy(blocks, blocks, g1r.at[half, dy]).wait()
        yy, a = (y + dy) % 2, along[half]
        send_line(half, yy, a, (a + 1) % 4)
        send_line(half, yy, a, (a + 3) % 4)

    def line_wait(half, yy, a):
        blocks = ga.at[pl.ds(half * NKV + line_pos(yy, a), 4), :, 0:ROWS]
        pltpu.make_async_copy(blocks, blocks, g2r.at[half, yy * 4 + a]).wait()
        blocks = ga.at[pl.ds(half * NKV + line_pos(yy, a), 4), within[half], ROWS:BLK]
        pltpu.make_async_copy(blocks, blocks, g3r.at[half, yy * 4 + a]).wait()

    first_wait(0, 0)
    first_wait(1, 0)

    lane = lax.broadcasted_iota(jnp.int32, (4 * ROWS, HD), 1)

    blank = jnp.zeros((4 * ROWS, HD), BF16)

    def coded(o):
        r = jnp.maximum(jnp.max(jnp.abs(o), axis=1, keepdims=True), 1e-30)
        inv = pl.reciprocal(r, approx=True) * CODE
        return jnp.round(o * inv).astype(jnp.int32).astype(I16), inv

    def packed(stats):
        total = stats[GH : 2 * GH]
        lse = stats[0:GH] * SCALE + jnp.log(total)
        return jnp.concatenate([lse, 1.0 / (stats[2 * GH : 3 * GH] * total)], axis=0)

    def noted(gl, lanes, m, total, inv, before):
        return jnp.where(
            lanes == gl, m, jnp.where(lanes == GH + gl, total, jnp.where(lanes == 2 * GH + gl, inv, before))
        )

    def send_to(src, dst, send_sem, recv_sem, to):
        pltpu.make_async_remote_copy(
            src_ref=src, dst_ref=dst, send_sem=send_sem, recv_sem=recv_sem, device_id=to, device_id_type=MESH
        ).start()

    def own_block(accs):
        def one(half, c):
            w = pick(half, within)
            col = lax.broadcasted_iota(jnp.int32, (4 * ROWS, NKV * 16), 1)
            row = lax.broadcasted_iota(jnp.int32, (4 * ROWS, NKV * 16), 0)
            p = col // 16
            src = jnp.where(half == 0, p, (p // 16) * 16 + (p % 4) * 4 + (p // 4) % 4)
            dst = device(half, y, pick(half, along), row // ROWS)
            allowed = (col % 16 < QB) & (src * QB + col % 16 <= dst * QB + row % QB)
            kv = ga[pl.ds(half * NKV, NKV), w, ROWS:BLK, :].reshape(NKV * 16, HD)
            q = ga[pl.ds(half * NKV + line_pos(y, pick(half, along)), 4), w, 0:ROWS, :].reshape(4 * ROWS, HD)
            tiles = [jnp.concatenate([kv[j * 256 : (j + 1) * 256], blank], axis=1) for j in range(2)]
            q = jnp.concatenate([q, blank], axis=1)
            for j in range(2):
                pltpu.matmul_push_rhs(tiles[j], j, 0, transpose=True)
                pltpu.matmul_acc_lhs(accs[j], q, load_staged_rhs=j)
            sc = jnp.concatenate([pltpu.matmul_pop(accs[0]), pltpu.matmul_pop(accs[1])], axis=1)
            sc = jnp.where(allowed, sc, LOW)
            m = jnp.max(sc, axis=1, keepdims=True)
            e = jnp.where(allowed, jnp.exp2((sc - m) * (SCALE * LOG2E)), 0.0)
            total = jnp.sum(e, axis=1, keepdims=True)
            e = pltpu.roll(e, 8, 1).astype(BF16)
            for j in range(2):
                pltpu.matmul_push_rhs(tiles[j], j, 1)
                pltpu.matmul_acc_lhs(accs[2], e[:, j * 256 : (j + 1) * 256], load_staged_rhs=j)
            code, inv = coded(pltpu.matmul_pop(accs[2])[:, 0:HD])
            bp[half] = code.reshape(4, ROWS, HD)
            inv2[...] = noted(w, lane, m, total, inv, jnp.ones((4 * ROWS, HD), F32))
            mine = lax.broadcasted_iota(jnp.int32, (8, HD), 0)
            for pair in range(2):
                flat = packed(inv2[pair * 2 * ROWS : (pair + 1) * 2 * ROWS, :].T)
                flat = jnp.where(mine % GH == w, flat, jnp.where(mine < GH, LOW, 0.0))
                ba[half, 2 * pair] = flat
                ba[half, 2 * pair + 1] = pltpu.roll(flat, ROWS, 1)
            return c

        lax.fori_loop(0, 2, one, 0)

    def join(half, dy):
        yy = (y + dy) % 2
        a, w = pick(half, along), pick(half, within)
        line = half * 2 + yy
        base = half * NKV + line_pos(yy, a)
        for k in range(3):
            got = r1.at[line, k]
            pltpu.make_async_copy(got, got, u1r.at[line, k]).wait()
            got = a1.at[line, k]
            pltpu.make_async_copy(got, got, b1r.at[line, k]).wait()
        notes = [pa[pl.ds(base, 4)]] + [a1[line, k] for k in range(3)] + ([ba[half]] if dy == 0 else [])
        top = functools.reduce(jnp.maximum, [n[:, 0:GH, :] for n in notes])
        lse = top + jnp.log(sum(jnp.exp(n[:, 0:GH, :] - top) for n in notes))
        blank = jnp.zeros((4, GH, HD), F32)
        factors = [
            jnp.concatenate([jnp.exp(n[:, 0:GH, :] - lse) * n[:, GH : 2 * GH, :], blank], axis=1).reshape(32, HD)
            for n in notes
        ]
        columns = jnp.concatenate(factors[0:4], axis=0).T
        if dy == 0:
            extra = jnp.concatenate([factors[4], jnp.zeros((HD - 32, HD), F32)], axis=0).T
        inv2[...] = jnp.ones((4 * ROWS, HD), F32)
        for gl in range(GH):
            for b in range(4):
                acc = None
                for i in range(len(notes)):
                    if i == 0:
                        part = po[base + b, gl]
                    elif i < 4:
                        part = r1[line, i - 1, b, gl]
                    else:
                        part = bp[half, b]
                    at = (i % 4) * 32 + b * 8 + gl
                    factor = (columns if i < 4 else extra)[0:ROWS, at : at + 1]
                    term = part.astype(jnp.int32).astype(F32) * factor
                    acc = term if acc is None else acc + term
                code, inv = coded(acc)
                po2[line, b, gl] = code
                inv2[b * ROWS : (b + 1) * ROWS, :] = jnp.where(lane[0:ROWS] == gl, inv, inv2[b * ROWS : (b + 1) * ROWS, :])
        for pair in range(2):
            scale = 1.0 / inv2[pair * 2 * ROWS : (pair + 1) * 2 * ROWS, :].T[0:GH, :]
            pa2[line, 2 * pair] = jnp.concatenate([lse[2 * pair], scale], axis=0)
            pa2[line, 2 * pair + 1] = jnp.concatenate([lse[2 * pair + 1], pltpu.roll(scale, ROWS, 1)], axis=0)
        for b in range(4):
            slot = half * SLOTS + y * 4 + w
            to = (nxt, device(half, yy, a, b))
            send_to(po2.at[line, b], rp.at[slot], u2s, u2r.at[half], to)
            send_to(pa2.at[line, b], ra.at[slot], b2s, b2r, to)

    def order(t):
        q = t // 2
        dy = jnp.where((q == 2) | (q == 3) | (q >= 6), 1, 0)
        off = jnp.where((q == 0) | (q == 7), 0, jnp.where((q == 1) | (q == 3), 3, jnp.where((q == 2) | (q == 4), 1, 2)))
        return t % 2, (y + dy) % 2, off

    def base_of(t):
        half, yy, off = order(t)
        return half * NKV + line_pos(yy, (jnp.where(half == 0, x, z) + off) % 4)

    def arrived(t):
        half, yy, off = order(t)
        q = t // 2

        @pl.when(t == 1)
        def _():
            first_wait(0, 1)
            first_wait(1, 1)

        @pl.when(t == 6)
        def _():
            residual.start()

        for h in range(2):
            a = along[h]

            @pl.when((t >= 2) & (t < 14) & (half == h))
            def _():
                line_wait(h, yy, (a + off) % 4)

                @pl.when(q == 1)
                def _():
                    send_line(h, y, (a + 3) % 4, (a + 1) % 4)

                @pl.when(q == 2)
                def _():
                    send_line(h, (y + 1) % 2, (a + 1) % 4, (a + 3) % 4)

    ss, pp = (s0, s1), (p0, p1)
    TILE, STEPS = 256, 8
    ones = jnp.where(lane == 0, 1.0, 0.0).astype(BF16)

    def scores_rhs(bases, gl):
        q = ga[pl.ds(bases[0], 4), gl, 0:ROWS, :].reshape(UROWS, HD)
        pltpu.matmul_push_rhs(jnp.concatenate([q, ones], axis=1), gl % 2, 0, transpose=True)

    def scores_lhs(j, g):
        rows = slice(j * TILE, (j + 1) * TILE)
        return jnp.concatenate([kraw[rows, pl.ds(pl.multiple_of(g * HD, HD), HD)], bias[rows, :]], axis=1)

    def values_push(j, buf):
        pltpu.matmul_push_rhs(pp[buf][j * TILE : (j + 1) * TILE, :], j % 2, 1)

    def values_lhs(j, g):
        return vt[g, :, j * TILE : (j + 1) * TILE]

    def scores_end(j, acc, buf):
        tile = pltpu.matmul_pop(acc)
        ss[buf][j * TILE : (j + 1) * TILE, :] = tile
        high = jnp.max(tile.reshape(TILE // 8, 8, UROWS), axis=0)
        mx[buf] = high if j == 0 else jnp.maximum(mx[buf], high)

    def softmax_chunk(j, m, total, buf):
        rows = slice(j * TILE, (j + 1) * TILE)
        w = jnp.exp2((ss[buf][rows, :] - m) * (SCALE * LOG2E))
        pp[buf][rows, :] = w.astype(BF16)
        added = jnp.sum(w.reshape(TILE // 8, 8, UROWS), axis=0)
        return added if total is None else total + added

    def softmax_end(m, total, gl, turn):
        total = jnp.sum(total, axis=0, keepdims=True)
        notes[turn, gl : gl + 1, :] = m * SCALE + jnp.log(total)
        notes[turn, 2 * GH + gl : 2 * GH + gl + 1, :] = total

    def values_end(o, bases, gl, turn):
        inv = CODE / jnp.maximum(jnp.max(jnp.abs(o), axis=0, keepdims=True), 1e-30)
        code = jnp.round((o * inv).T).astype(jnp.int32).astype(I16)
        po[pl.ds(bases[0], 4), gl] = code.reshape(4, ROWS, HD)
        notes[turn, GH + gl : GH + gl + 1, :] = 1.0 / (inv * notes[turn, 2 * GH + gl : 2 * GH + gl + 1, :])

    def step(accs, after, now, before, pending):
        gl = now[3]
        buf, other = gl % 2, 1 - gl % 2
        score, value = accs[0:2], accs[3 + other]
        g_a, g_b = after[1] * GH + after[3], before[1] * GH + before[3]
        scores_rhs(after[0], after[3])
        values_push(0, other)
        m = total = None
        for j in range(STEPS):
            pltpu.matmul_acc_lhs(score[j % 2], scores_lhs(j, g_a), load_staged_rhs=after[3] % 2 if j == 0 else None)
            pltpu.matmul_acc_lhs(value, values_lhs(j, g_b), load_staged_rhs=j % 2)
            if j == 0:
                for todo in pending:
                    todo()
                m = jnp.max(mx[buf], axis=0, keepdims=True)
            if j + 1 < STEPS:
                values_push(j + 1, other)
            total = softmax_chunk(j, m, total, buf)
            if j > 0:
                scores_end(j - 1, score[(j - 1) % 2], other)
        softmax_end(m, total, gl, now[2])

        def last_tile():
            scores_end(STEPS - 1, score[(STEPS - 1) % 2], other)

        def values():
            values_end(pltpu.matmul_pop(value), before[0], before[3], before[2])

        return last_tile, values

    def pack_notes(bases, turn):
        for pair in range(2):
            flat = notes[turn, 0 : 2 * GH, pair * HD : (pair + 1) * HD]
            pa[bases[0] + 2 * pair] = flat
            pa[bases[0] + 2 * pair + 1] = pltpu.roll(flat, ROWS, 1)

    def send_unit(t):
        half, yy, off = order(t)
        base = base_of(t)
        line = half * 2 + yy
        k = jnp.where(off == 2, 2, off // 2)
        to = (s, device(half, y, (pick(half, along) + off) % 4, pick(half, within)))

        @pl.when((t >= 0) & (off != 0))
        def _():
            blocks = pl.ds(base, 4)
            send_to(po.at[blocks], r1.at[line, k], u1s, u1r.at[line, k], to)
            send_to(pa.at[blocks], a1.at[line, k], b1s, b1r.at[line, k], to)

    def unit(accs, t, c):
        arrived(t)
        send_unit(t - 2)

        @pl.when(t == 14)
        def _():
            own_block(accs)

        @pl.when(t == 15)
        def _():
            def both(half, c2):
                join(half, 0)
                return c2

            lax.fori_loop(0, 2, both, 0)

        tb = jnp.maximum(t - 1, 0)
        new = lambda gl: ((base_of(t),), t % 2, t % 2, gl)
        old = lambda gl: ((base_of(tb),), tb % 2, (t + 1) % 2, gl)
        todo = step(accs, new(0), old(3), old(2), ())
        todo = step(accs, new(1), new(0), old(3), todo)
        todo = step(accs, new(2), new(1), new(0), todo)
        pack_notes((base_of(tb),), (t + 1) % 2)
        todo = step(accs, new(3), new(2), new(1), todo)
        for last in todo:
            last()
        return c

    load_k.wait()
    for ref in (p0, p1):
        ref[...] = jnp.zeros((CTX, UROWS), BF16)
    s1[...] = jnp.zeros((CTX, UROWS), F32)
    mx[...] = jnp.zeros((2, 8, UROWS), F32)
    notes[...] = jnp.ones((2, 16, UROWS), F32)

    def units(*accs):
        lax.fori_loop(0, 16, functools.partial(unit, accs), 0)
        bases, value = (base_of(15),), accs[3]
        m, total = jnp.max(mx[1], axis=0, keepdims=True), None
        for j in range(STEPS):
            values_push(j, 0)
            pltpu.matmul_acc_lhs(value, values_lhs(j, 6), load_staged_rhs=j % 2)
            total = softmax_chunk(j, m, total, 1)
        softmax_end(m, total, 3, 1)
        values_end(pltpu.matmul_pop(value), bases, 2, 1)
        for j in range(STEPS):
            values_push(j, 1)
            pltpu.matmul_acc_lhs(value, values_lhs(j, 7), load_staged_rhs=j % 2)
        values_end(pltpu.matmul_pop(value), bases, 3, 1)

    shapes = ((0, UROWS), (0, UROWS), (1, UROWS), (1, HD), (1, HD))
    pl.run_scoped(units, *(pltpu.ACC(one)((size, 2 * HD), F32) for one, size in shapes))
    join(0, 1)
    pack_notes((base_of(15),), 1)
    join(1, 1)

    pltpu.make_async_copy(ra, ra, b2r).wait()
    cols = lax.broadcasted_iota(jnp.int32, (QB, HD), 1)
    lout = jnp.zeros((QB, HD), F32)
    for half in range(2):
        lses = ra[half * SLOTS : (half + 1) * SLOTS, 0:GH, :]
        top = jnp.max(lses, axis=0, keepdims=True)
        lse = top + jnp.log(jnp.sum(jnp.exp(lses - top), axis=0, keepdims=True))
        ra[half * SLOTS : (half + 1) * SLOTS, 0:GH, :] = (
            jnp.exp(lses - lse) * ra[half * SLOTS : (half + 1) * SLOTS, GH : 2 * GH, :]
        )
        flat = jnp.concatenate([lse[0], jnp.zeros((HD - GH, HD), F32)], axis=0).T
        for gl in range(GH):
            for h in range(8):
                piece = flat[h * QB : (h + 1) * QB, gl : gl + 1]
                lout = jnp.where(cols == (half * GH + gl) * 8 + h, piece, lout)
    lsend[...] = lout
    back = pltpu.make_async_remote_copy(
        src_ref=lsend, dst_ref=lrecv, send_sem=lss, recv_sem=lsr, device_id=(prv, me), device_id_type=MESH
    )
    back.start()
    residual.wait_recv()

    for half in range(2):
        parts = rp.at[pl.ds(half * SLOTS, SLOTS)]
        pltpu.make_async_copy(parts, parts, u2r.at[half]).wait()

        f = ra[half * SLOTS : (half + 1) * SLOTS].reshape(SLOTS * 8, HD)
        factors = jnp.concatenate([f, jnp.zeros((HD - SLOTS * 8, HD), F32)], axis=0).T
        acc = [None] * GH
        for i in range(SLOTS):
            for gl in range(GH):
                part = rp[half * SLOTS + i, gl].astype(jnp.int32).astype(F32)
                part = part * factors[0:ROWS, i * 8 + gl : i * 8 + gl + 1]
                acc[gl] = part if i == 0 else acc[gl] + part
        for gl in range(GH):
            for h in range(8):
                c0 = ((half * GH + gl) * 8 + h) * HD
                out_ref[:, c0 : c0 + HD] = rres[:, c0 : c0 + HD] + acc[gl][h * QB : (h + 1) * QB, :]

    back.wait_recv()
    lse_ref[...] = lrecv[:, 0:HQ]
    back.wait_send()
    residual.wait_send()
    blocks = ga.at[pl.ds(0, 14)]
    pltpu.make_async_copy(blocks, blocks, g1s).wait()
    blocks = ga.at[pl.ds(0, 48), :, 0:ROWS]
    pltpu.make_async_copy(blocks, blocks, g2s).wait()
    blocks = ga.at[pl.ds(0, 48), 0, ROWS:BLK]
    pltpu.make_async_copy(blocks, blocks, g3s).wait()
    for ref, sem in ((po.at[pl.ds(0, 48)], u1s), (pa.at[pl.ds(0, 48)], b1s), (po2, u2s), (pa2, b2s)):
        pltpu.make_async_copy(ref, ref, sem).wait()


def per_device(queries, cache_keys, cache_values, new_keys, new_values, lengths, residual):
    vmem = pl.BlockSpec(memory_space=pltpu.VMEM)
    hbm = pl.BlockSpec(memory_space=pl.ANY)
    dma = pltpu.SemaphoreType.DMA
    handed, lse = pl.pallas_call(
        kernel,
        out_shape=(jax.ShapeDtypeStruct((QB, HQ * HD), F32), jax.ShapeDtypeStruct((QB, HQ), F32)),
        in_specs=[pl.BlockSpec(memory_space=pltpu.SMEM), vmem, vmem, vmem, vmem, hbm, hbm],
        out_specs=(vmem, vmem),
        scratch_shapes=[
            pltpu.VMEM((2 * NKV, GH, BLK, HD), BF16),
            pltpu.VMEM((CTX, KVH * HD), BF16),
            pltpu.VMEM((KVH, HD, CTX), BF16),
            pltpu.VMEM((CTX, KVH * HD), BF16),
            pltpu.VMEM((CTX, HD), BF16),
            pltpu.VMEM((2 * NKV, GH, ROWS, HD), I16),
            pltpu.VMEM((2 * NKV, 8, HD), F32),
            pltpu.VMEM((4, 3, 4, GH, ROWS, HD), I16),
            pltpu.VMEM((4, 3, 4, 8, HD), F32),
            pltpu.VMEM((2, 4, ROWS, HD), I16),
            pltpu.VMEM((2, 4, 8, HD), F32),
            pltpu.VMEM((4, 4, GH, ROWS, HD), I16),
            pltpu.VMEM((4, 4, 8, HD), F32),
            pltpu.VMEM((2 * SLOTS, GH, ROWS, HD), I16),
            pltpu.VMEM((2 * SLOTS, 8, HD), F32),
            pltpu.VMEM((QB, HQ * HD), F32),
            pltpu.VMEM((QB, HQ * HD), F32),
            pltpu.VMEM((QB, HD), F32),
            pltpu.VMEM((QB, HD), F32),
            pltpu.VMEM((2, 16, UROWS), F32),
            pltpu.VMEM((4 * ROWS, HD), F32),
            pltpu.VMEM((CTX, UROWS), F32),
            pltpu.VMEM((CTX, UROWS), F32),
            pltpu.VMEM((CTX, UROWS), BF16),
            pltpu.VMEM((CTX, UROWS), BF16),
            pltpu.VMEM((2, 8, UROWS), F32),
            dma((2,)),
            dma,
            dma((2, 2)),
            dma,
            dma((2, 8)),
            dma,
            dma((2, 8)),
            dma,
            dma((4, 3)),
            dma,
            dma((4, 3)),
            dma,
            dma((2,)),
            dma,
            dma,
            dma,
            dma,
            dma,
            dma,
        ],
        compiler_params=pltpu.CompilerParams(
            collective_id=0, has_side_effects=True, vmem_limit_bytes=60 * 1024 * 1024
        ),
        cost_estimate=pl.CostEstimate(
            flops=4 * HQ * 256 * CTX * HD, bytes_accessed=12 * 1024 * 1024, transcendentals=HQ * 256 * CTX
        ),
    )(lengths, queries[0], new_keys[0], new_values[0], residual[0], cache_keys[0], cache_values[0])
    return handed[None], lse[None]


def solution(mesh):
    rows = P("section", "kv", None)
    return jax.shard_map(
        per_device,
        mesh=mesh,
        in_specs=(rows, rows, rows, rows, rows, P("section", "kv"), rows),
        out_specs=(rows, rows),
        check_vma=False,
    )
```
